32 devices in a mesh: segment: 4 (over y, x), tensor: 8 (over z, core).
Axes of the slice: x: 2, y: 2, z: 4, core: 2. Of those that a mesh axis runs over, the one named last changes fastest.
Arguments:
- hidden: bfloat16 [4, 2, 768, 3072], P('segment', None, 'tensor'), may hold values from -6 to 6
- gate_weight: bfloat16 [4, 3072, 4096], P('segment', None, 'tensor'), may hold values from -0.109375 to 0.109375
- up_weight: bfloat16 [4, 3072, 4096], P('segment', None, 'tensor'), may hold values from -0.109375 to 0.109375
- down_weight: bfloat16 [4, 4096, 3072], P('segment', 'tensor'), may hold values from -0.09375 to 0.09375
- block_rows: int32 [4, 2, 6, 128], P('segment'), may hold values from 0 to 768, as said below
- slot_gate: float32 [4, 2, 6, 128], P('segment'), may hold values from 0.1 to 1
Outputs:
- handed: bfloat16 [4, 2, 768, 3072], P('segment', None, 'tensor')
The draws below stay inside these ranges and needn't reach their ends.
Inputs may be any that keep to these rules, and one draw needn't show every extreme that they name: `block_rows`: each entry is a token row of its micro-batch or 768 for an empty slot. Within one list of 768 slots the named rows are distinct and ascending and the empty slots come last; a list holds from 307 to 768 live slots, and both ends occur in every draw.
All inputs are finite; a program needn't handle non-finite values.
Results may differ from the reference program's by a relative error of at most 0.0085.
Values may be sent and summed in bfloat16 or wider, within the bound.
No kernel may reach another device: no remote copies, remote signals or barrier semaphores. Data moves between devices by JAX's collectives and lax.ppermute only.
A program may use at most 128 MiB of HBM per device.

```python
import jax
import jax.numpy as jnp
from jax import lax

D = 3072
FF_DEV = 512
FF = 4096
M = 768
MB = 2
BLOCK = 128
NB = 6
SLOTS = 768
N_SEGMENT = 4
N_TENSOR = 8


def draw_block_rows(key, part):
    list_count = N_SEGMENT * MB
    key_list = jax.random.split(key, list_count)
    lowest = 2 * SLOTS // 5

    def draw_one(sub_key, position):
        first_key, second_key = jax.random.split(sub_key)
        live_count = jax.random.randint(first_key, (), lowest, SLOTS + 1)
        live_count = jnp.where(position == 0, SLOTS, live_count)
        live_count = jnp.where(position == MB, lowest, live_count)
        shuffled = jax.random.permutation(second_key, M)[:SLOTS]
        slot_ids = jnp.arange(SLOTS)
        picked = jnp.where(slot_ids < live_count, shuffled, M)
        return jnp.sort(picked).astype(jnp.int32)
    all_lists = jax.vmap(draw_one)(key_list, jnp.arange(list_count))
    return all_lists.reshape(N_SEGMENT, MB, NB, BLOCK)


def level_of(own_key, extent, cuts, smallest, top_value):
    def one(axis_at, parts):
        heights = jax.random.uniform(jax.random.fold_in(jax.random.fold_in(own_key, 6), axis_at), (parts,), jnp.float32, smallest / len(cuts), top_value / len(cuts))
        return jnp.repeat(jnp.exp(heights), extent[axis_at] // parts).reshape((-1,) + (1,) * (len(extent) - axis_at - 1))

    factor_of = one(*cuts[0])
    for cut in cuts[1:]:
        factor_of = factor_of * one(*cut)
    return factor_of


def scatter_about(key, shape, scale, reach, shards=(), held_as=jnp.bfloat16):
    array = scale * jax.random.normal(key, shape, jnp.float32)
    if shards:
        array = array * level_of(key, shape, shards, -0.22, 0.18)
    return jnp.clip(array, -reach, reach).astype(held_as)


def setup_inputs(seed: int = 0) -> dict:
    seeds = jax.random.split(jax.random.key(seed), 7)
    hidden = scatter_about(seeds[0], (N_SEGMENT, MB, M, D), 1.0, 6.0, ((0, 4), (2, 8)))
    gate_weight = scatter_about(seeds[1], (N_SEGMENT, D, FF), D ** -0.5, 0.109375, ((0, 4), (2, 8)))
    up_weight = scatter_about(seeds[2], (N_SEGMENT, D, FF), D ** -0.5, 0.109375, ((0, 4), (2, 8)))
    down_weight = scatter_about(seeds[3], (N_SEGMENT, FF, D), FF ** -0.5, 0.09375, ((0, 4), (1, 8)))
    block_rows = draw_block_rows(jax.random.fold_in(seeds[6], 71), 0)
    slot_gate = jnp.clip(0.1 + 0.9 * jax.random.uniform(seeds[5], (N_SEGMENT, MB, NB, BLOCK), jnp.float32) ** level_of(seeds[5], (N_SEGMENT, MB, NB, BLOCK), ((0, 4),), -0.2, 0.2), 0.1, 1.0)
    return {"hidden": hidden, "gate_weight": gate_weight, "up_weight": up_weight, "down_weight": down_weight, "block_rows": block_rows, "slot_gate": slot_gate}


def expert_phase(inputs):
    hidden, gate_weight, up_weight, down_weight, block_rows, slot_gate = inputs
    outputs = []
    for micro_batch in range(MB):
        tokens_in = hidden[micro_batch]
        padded = jnp.concatenate([tokens_in, jnp.zeros((1, D), tokens_in.dtype)], axis=0)
        indices = block_rows[micro_batch].reshape(SLOTS).astype(jnp.int32)
        slot_in = padded[indices]
        gate_act = jnp.dot(slot_in, gate_weight, preferred_element_type=jnp.float32)
        up_act = jnp.dot(slot_in, up_weight, preferred_element_type=jnp.float32)
        hidden_act = (jax.nn.silu(gate_act) * up_act).astype(jnp.bfloat16)
        grouped_act = hidden_act.reshape(SLOTS, N_TENSOR, FF_DEV).astype(jnp.float32)
        grouped_down = down_weight.reshape(N_TENSOR, FF_DEV, D).astype(jnp.float32)
        partial_value = jnp.einsum("sgf,gfd->gsd", grouped_act, grouped_down)
        gate_column = slot_gate[micro_batch].reshape(1, SLOTS, 1)
        rounded = (partial_value * gate_column).astype(jnp.bfloat16)
        rounded = lax.optimization_barrier(rounded)
        summed = jnp.sum(rounded.astype(jnp.float32), axis=0)
        placed = jnp.zeros((M + 1, D), jnp.float32).at[indices].add(summed)[:M]
        outputs.append((tokens_in.astype(jnp.float32) + placed).astype(jnp.bfloat16))
    return jnp.stack(outputs)


def reference(hidden, gate_weight, up_weight, down_weight, block_rows, slot_gate):
    phase_out = lax.map(expert_phase, (hidden, gate_weight, up_weight, down_weight, block_rows, slot_gate))
    return jnp.roll(phase_out, 1, axis=0)
```

```python
import functools

import jax
import jax.numpy as jnp
from jax import lax
from jax.experimental import pallas as pl
from jax.experimental.pallas import tpu as pltpu
from jax.sharding import PartitionSpec as P

CORES = 2
CHIPS = 4
BF16 = jnp.bfloat16
F32 = jnp.float32

NEAR = [(0, 1), (1, 0), (2, 3), (3, 2)]
MIDDLE = [(1, 2), (2, 1)]
OUTWARD = [(1, 0), (2, 3)]
INWARD = [(0, 1), (3, 2)]
STAY = [(0, 0), (1, 1), (2, 2), (3, 3)]


def along_line(value, pairs):
    full = [(CORES * a + c, CORES * b + c) for a, b in pairs for c in range(CORES)]
    return lax.ppermute(value, "tensor", full)


def across_cores(value):
    count = lax.axis_size("tensor")
    return lax.ppermute(value, "tensor", [(i, i ^ 1) for i in range(count)])


def to_next_phase(value, pairs, cross):
    segments, count = lax.axis_size("segment"), lax.axis_size("tensor")
    full = [
        (s * count + CORES * a + c, ((s + 1) % segments) * count + CORES * b + (c ^ cross))
        for s in range(segments)
        for a, b in pairs
        for c in range(CORES)
    ]
    return lax.ppermute(value, ("segment", "tensor"), full)


def ffn_kernel(layout, *refs):
    n_in = sum(choices for _, choices in layout)
    n_out = len(layout)
    meta, slot_rows, slot_gates = refs[:3]
    x_refs = refs[3 : 3 + n_in]
    weights = refs[3 + n_in : 9 + n_in]
    outs = refs[9 + n_in : 9 + n_in + n_out]
    x, h, gate, wg, wu, wd, sem_g, sem_u, sem_d = refs[9 + n_in + n_out :]
    tiles, _, width = wg.shape
    columns, _, out_width = wd.shape
    per_core = tiles // CORES
    deep = per_core * width

    copies_in, copies_out = [], []
    for tile in range(tiles):
        core, part = tile // per_core, tile % per_core
        span = pl.ds(part * width, width)
        g = pltpu.make_async_copy(weights[3 * core].at[:, span], wg.at[tile], sem_g.at[tile])
        u = pltpu.make_async_copy(weights[3 * core + 1].at[:, span], wu.at[tile], sem_u.at[tile])
        g.start()
        u.start()
        copies_in.append((g, u))
    for column in range(columns):
        pair = []
        for core in range(CORES):
            d = pltpu.make_async_copy(
                weights[3 * core + 2].at[:, pl.ds(column * out_width, out_width)],
                wd.at[column, pl.ds(core * deep, deep)],
                sem_d.at[column, core],
            )
            d.start()
            pair.append(d)
        copies_out.append(pair)

    second = meta[0] == 1
    start, at = 0, 0
    for block, (rows, choices) in enumerate(layout):
        here = pl.ds(start, rows)
        if choices == 1:
            x[here, :] = x_refs[at][...]
        else:
            first_ref, second_ref = x_refs[at], x_refs[at + 1]

            @pl.when(second)
            def _(here=here, ref=second_ref):
                x[here, :] = ref[...]

            @pl.when(jnp.logical_not(second))
            def _(here=here, ref=first_ref):
                x[here, :] = ref[...]

        half_rows = rows // CORES
        for half in range(CORES):
            tokens = meta[1 + CORES * block + half] + lax.broadcasted_iota(
                jnp.int32, (half_rows, slot_rows.shape[1]), 0
            )
            named = jnp.where(slot_rows[...] == tokens, slot_gates[...], 0.0)
            column = jnp.sum(named, axis=1, keepdims=True)
            gate[pl.ds(start + half * half_rows, half_rows), :] = jnp.broadcast_to(
                column, (half_rows, gate.shape[1])
            )
        start += rows
        at += choices

    for tile in range(tiles):
        for copy in copies_in[tile]:
            copy.wait()
        g = jnp.dot(x[...], wg[tile], preferred_element_type=F32)
        u = jnp.dot(x[...], wu[tile], preferred_element_type=F32)
        h[:, tile * width : (tile + 1) * width] = (g / (1.0 + jnp.exp(-g)) * u).astype(BF16)
    for column in range(columns):
        for copy in copies_out[column]:
            copy.wait()
        span = slice(column * out_width, (column + 1) * out_width)
        y = jnp.dot(h[...], wd[column], preferred_element_type=F32)
        y = (y * gate[:, :1]).astype(BF16)
        start = 0
        for (rows, _), out in zip(layout, outs):
            out[:, span] = y[start : start + rows, :]
            start += rows


def ffn(meta, slot_rows, slot_gates, blocks, weights):
    layout = tuple((block[0].shape[0], len(block)) for block in blocks)
    features, hidden_units = weights[0].shape
    total = sum(rows for rows, _ in layout)
    width = 256 if hidden_units % 256 == 0 else hidden_units
    tiles = CORES * hidden_units // width
    out_width = 768 if features % 768 == 0 else features
    columns = features // out_width
    any_space = pl.BlockSpec(memory_space=pl.ANY)
    vmem = pl.BlockSpec(memory_space=pltpu.VMEM)
    flat = [choice for block in blocks for choice in block]
    return pl.pallas_call(
        functools.partial(ffn_kernel, layout),
        out_shape=[jax.ShapeDtypeStruct((rows, features), BF16) for rows, _ in layout],
        in_specs=[pl.BlockSpec(memory_space=pltpu.SMEM), vmem, vmem]
        + [vmem] * len(flat)
        + [any_space] * 6,
        out_specs=[vmem] * len(layout),
        scratch_shapes=[
            pltpu.VMEM((total, features), BF16),
            pltpu.VMEM((total, CORES * hidden_units), BF16),
            pltpu.VMEM((total, 128), F32),
            pltpu.VMEM((tiles, features, width), BF16),
            pltpu.VMEM((tiles, features, width), BF16),
            pltpu.VMEM((columns, CORES * hidden_units, out_width), BF16),
            pltpu.SemaphoreType.DMA((tiles,)),
            pltpu.SemaphoreType.DMA((tiles,)),
            pltpu.SemaphoreType.DMA((columns, CORES)),
        ],
        compiler_params=pltpu.CompilerParams(vmem_limit_bytes=44 * 1024 * 1024),
        cost_estimate=pl.CostEstimate(
            flops=12 * total * features * hidden_units,
            bytes_accessed=12 * features * hidden_units,
            transcendentals=total * CORES * hidden_units,
        ),
    )(meta, slot_rows, slot_gates, *flat, *weights)


def add(*values):
    return sum(value.astype(F32) for value in values).astype(BF16)


def staged(hidden, gate_weight, up_weight, down_weight, block_rows, slot_gate, chunks):
    rows_here, features = hidden.shape[2], hidden.shape[3]
    slots = block_rows.shape[2] * block_rows.shape[3]
    index = lax.axis_index("tensor")
    core, chip = index % CORES, index // CORES
    right = chip >= CHIPS // 2
    inner = jnp.logical_and(chip > 0, chip < CHIPS - 1)

    mine = lax.dynamic_index_in_dim(hidden[0], core, 0, keepdims=False)
    theirs = lax.dynamic_index_in_dim(hidden[0], 1 - core, 0, keepdims=False)
    slot_rows = lax.dynamic_index_in_dim(block_rows[0], core, 0, keepdims=False).reshape(1, slots)
    slot_gates = lax.dynamic_index_in_dim(slot_gate[0], core, 0, keepdims=False).reshape(1, slots)

    other = across_cores(theirs)
    other, *own_weights = lax.optimization_barrier(
        (other, gate_weight[0], up_weight[0], down_weight[0])
    )
    weights = own_weights + [across_cores(weight) for weight in own_weights]

    spans, start = [], 0
    for size in chunks:
        spans.append((start, size))
        start += size

    def token(mirrored_block, half, offset):
        block = jnp.where(right, CHIPS - 1 - mirrored_block, mirrored_block)
        owner = block * CORES + jnp.where(half == 0, core, 1 - core)
        return owner * rows_here + offset

    def meta_of(blocks, flag):
        values = [flag.astype(jnp.int32)]
        for mirrored_block, offset in blocks:
            values += [token(mirrored_block, half, offset) for half in range(CORES)]
        return jnp.stack(values).astype(jnp.int32)

    own_block = inner.astype(jnp.int32)
    near_block = 1 - own_block

    own = jnp.concatenate([mine, other], axis=0)
    pieces = [
        jnp.concatenate([mine[o : o + n], other[o : o + n]], axis=0) for o, n in spans
    ]

    near = along_line(own, NEAR)
    second_at_inner = [along_line(piece, MIDDLE) for piece in pieces]
    second_at_outer = [along_line(piece, OUTWARD) for piece in second_at_inner]
    near_pieces = [
        jnp.concatenate(
            [near[o : o + n], near[rows_here + o : rows_here + o + n]], axis=0
        )
        for o, n in spans
    ]
    third_at_inner = [along_line(piece, MIDDLE) for piece in near_pieces]
    third_at_outer = [along_line(piece, OUTWARD) for piece in third_at_inner]

    own_part, near_part = ffn(
        meta_of([(own_block, 0), (near_block, 0)], jnp.int32(0)),
        slot_rows,
        slot_gates,
        [(own,), (near,)],
        weights,
    )
    from_end = along_line(near_part, INWARD)

    base = add(own, own_part, from_end)
    base_same = to_next_phase(base[:rows_here], STAY, 0)
    base_cross = to_next_phase(base[rows_here:], STAY, 1)

    same, cross = [], []
    for (o, n), a2, b2, a3, b3 in zip(
        spans, second_at_outer, second_at_inner, third_at_outer, third_at_inner
    ):
        part2, part3 = ffn(
            meta_of([(2, o), (3, o)], inner),
            slot_rows,
            slot_gates,
            [(a2, b2), (a3, b3)],
            weights,
        )
        sum3 = add(part3, along_line(part3, INWARD))
        sum2 = add(part2, along_line(part2, INWARD))
        over = along_line(sum3, MIDDLE)
        for_end = add(
            jnp.concatenate(
                [near_part[o : o + n], near_part[rows_here + o : rows_here + o + n]], axis=0
            ),
            over,
        )
        got_same = [base_same[o : o + n]]
        got_cross = [base_cross[o : o + n]]
        for value, pairs in ((sum2, MIDDLE), (for_end, OUTWARD)):
            got_same.append(to_next_phase(value[:n], pairs, 0))
            got_cross.append(to_next_phase(value[n:], pairs, 1))
        same.append(add(*got_same))
        cross.append(add(*got_cross))
    same = jnp.concatenate(same, axis=0)
    cross = jnp.concatenate(cross, axis=0)
    low = core == 0
    return jnp.stack([jnp.where(low, same, cross), jnp.where(low, cross, same)])[None]


def whole_gather(hidden, gate_weight, up_weight, down_weight, block_rows, slot_gate):
    rows_here = hidden.shape[2]
    slots = block_rows.shape[2] * block_rows.shape[3]
    total_rows = rows_here * lax.axis_size("tensor")
    gathered = lax.all_gather(hidden, "tensor", axis=2, tiled=True)
    results = []
    for micro_batch in range(hidden.shape[1]):
        x = gathered[0, micro_batch]
        slot_rows = block_rows[0, micro_batch].reshape(1, slots)
        slot_gates = slot_gate[0, micro_batch].reshape(1, slots)
        tokens = lax.broadcasted_iota(jnp.int32, (total_rows, 1), 0)
        gate = jnp.sum(jnp.where(slot_rows == tokens, slot_gates, 0.0), axis=1, keepdims=True)
        gate_act = jnp.dot(x, gate_weight[0], preferred_element_type=F32)
        up_act = jnp.dot(x, up_weight[0], preferred_element_type=F32)
        hidden_act = (jax.nn.silu(gate_act) * up_act).astype(BF16)
        part = jnp.dot(hidden_act, down_weight[0], preferred_element_type=F32) * gate
        placed = lax.psum_scatter(
            part.astype(BF16), "tensor", scatter_dimension=0, tiled=True
        )
        results.append(add(hidden[0, micro_batch], placed))
    count = lax.axis_size("segment")
    pairs = [(source, (source + 1) % count) for source in range(count)]
    return lax.ppermute(jnp.stack(results)[None], "segment", pairs)


def per_device(*args):
    rows_here = args[0].shape[2]
    if (
        lax.axis_size("tensor") != CORES * CHIPS
        or args[0].shape[1] != CORES
        or rows_here % 32 != 0
    ):
        return whole_gather(*args)
    return staged(*args, chunks=CHUNKS(rows_here))


def CHUNKS(rows):
    return [rows // 2, rows // 2]


def solution(mesh):
    return jax.shard_map(
        per_device,
        mesh=mesh,
        in_specs=(
            P("segment", None, "tensor", None),
            P("segment", None, "tensor"),
            P("segment", None, "tensor"),
            P("segment", "tensor", None),
            P("segment", None, None, None),
            P("segment", None, None, None),
        ),
        out_specs=P("segment", None, "tensor", None),
        check_vma=False,
    )
```

```python
import functools

import jax
import jax.numpy as jnp
from jax import lax
from jax.experimental import pallas as pl
from jax.experimental.pallas import tpu as pltpu
from jax.sharding import PartitionSpec as P

CORES = 2
CHIPS = 4
BF16 = jnp.bfloat16
F32 = jnp.float32

NEAR = [(0, 1), (1, 0), (2, 3), (3, 2)]
MIDDLE = [(1, 2), (2, 1)]
OUTWARD = [(1, 0), (2, 3)]
INWARD = [(0, 1), (3, 2)]
ENDS = [(0, 0), (3, 3)]
STAY = [(0, 0), (1, 1), (2, 2), (3, 3)]


def along_line(value, pairs):
    full = [(CORES * a + c, CORES * b + c) for a, b in pairs for c in range(CORES)]
    return lax.ppermute(value, "tensor", full)


def across_cores(value):
    count = lax.axis_size("tensor")
    return lax.ppermute(value, "tensor", [(i, i ^ 1) for i in range(count)])


def to_next_phase(value, pairs, cross):
    segments, count = lax.axis_size("segment"), lax.axis_size("tensor")
    full = [
        (s * count + CORES * a + c, ((s + 1) % segments) * count + CORES * b + (c ^ cross))
        for s in range(segments)
        for a, b in pairs
        for c in range(CORES)
    ]
    return lax.ppermute(value, ("segment", "tensor"), full)


def ffn_kernel(layout, out_rows, *refs):
    n_in = sum(choices for _, choices in layout)
    n_out = len(out_rows)
    meta, slot_rows, slot_gates = refs[:3]
    x_refs = refs[3 : 3 + n_in]
    weights = refs[3 + n_in : 9 + n_in]
    outs = refs[9 + n_in : 9 + n_in + n_out]
    x, h, gate, wg, wu, wd, sem_g, sem_u, sem_d = refs[9 + n_in + n_out :]
    tiles, _, width = wg.shape
    columns, _, out_width = wd.shape
    per_core = tiles // CORES
    deep = per_core * width

    copies_in, copies_out = [], []
    for tile in range(tiles):
        core, part = tile // per_core, tile % per_core
        span = pl.ds(part * width, width)
        g = pltpu.make_async_copy(weights[3 * core].at[:, span], wg.at[tile], sem_g.at[tile])
        u = pltpu.make_async_copy(weights[3 * core + 1].at[:, span], wu.at[tile], sem_u.at[tile])
        g.start()
        u.start()
        copies_in.append((g, u))
    for column in range(columns):
        pair = []
        for core in range(CORES):
            d = pltpu.make_async_copy(
                weights[3 * core + 2].at[:, pl.ds(column * out_width, out_width)],
                wd.at[column, pl.ds(core * deep, deep)],
                sem_d.at[column, core],
            )
            d.start()
            pair.append(d)
        copies_out.append(pair)

    second = meta[0] == 1
    start, at = 0, 0
    for block, (rows, choices) in enumerate(layout):
        here = pl.ds(start, rows)
        if choices == 1:
            x[here, :] = x_refs[at][...]
        else:
            first_ref, second_ref = x_refs[at], x_refs[at + 1]

            @pl.when(second)
            def _(here=here, ref=second_ref):
                x[here, :] = ref[...]

            @pl.when(jnp.logical_not(second))
            def _(here=here, ref=first_ref):
                x[here, :] = ref[...]

        tokens = meta[1 + block] + lax.broadcasted_iota(
            jnp.int32, (rows, slot_rows.shape[1]), 0
        )
        named = jnp.where(slot_rows[...] == tokens, slot_gates[...], 0.0)
        column = jnp.sum(named, axis=1, keepdims=True)
        gate[here, :] = jnp.broadcast_to(column, (rows, gate.shape[1]))
        start += rows
        at += choices

    for tile in range(tiles):
        for copy in copies_in[tile]:
            copy.wait()
        g = jnp.dot(x[...], wg[tile], preferred_element_type=F32)
        u = jnp.dot(x[...], wu[tile], preferred_element_type=F32)
        h[:, tile * width : (tile + 1) * width] = (g / (1.0 + jnp.exp(-g)) * u).astype(BF16)
    for column in range(columns):
        for copy in copies_out[column]:
            copy.wait()
        span = slice(column * out_width, (column + 1) * out_width)
        y = jnp.dot(h[...], wd[column], preferred_element_type=F32)
        y = (y * gate[:, :1]).astype(BF16)
        start = 0
        for rows, out in zip(out_rows, outs):
            out[:, span] = y[start : start + rows, :]
            start += rows


def ffn(meta, slot_rows, slot_gates, blocks, weights, out_rows):
    layout = tuple((block[0].shape[0], len(block)) for block in blocks)
    features, hidden_units = weights[0].shape
    total = sum(rows for rows, _ in layout)
    width = 256 if hidden_units % 256 == 0 else hidden_units
    tiles = CORES * hidden_units // width
    out_width = 768 if features % 768 == 0 else features
    columns = features // out_width
    any_space = pl.BlockSpec(memory_space=pl.ANY)
    vmem = pl.BlockSpec(memory_space=pltpu.VMEM)
    flat = [choice for block in blocks for choice in block]
    return pl.pallas_call(
        functools.partial(ffn_kernel, layout, out_rows),
        out_shape=[jax.ShapeDtypeStruct((rows, features), BF16) for rows in out_rows],
        in_specs=[pl.BlockSpec(memory_space=pltpu.SMEM), vmem, vmem]
        + [vmem] * len(flat)
        + [any_space] * 6,
        out_specs=[vmem] * len(out_rows),
        scratch_shapes=[
            pltpu.VMEM((total, features), BF16),
            pltpu.VMEM((total, CORES * hidden_units), BF16),
            pltpu.VMEM((total, 128), F32),
            pltpu.VMEM((tiles, features, width), BF16),
            pltpu.VMEM((tiles, features, width), BF16),
            pltpu.VMEM((columns, CORES * hidden_units, out_width), BF16),
            pltpu.SemaphoreType.DMA((tiles,)),
            pltpu.SemaphoreType.DMA((tiles,)),
            pltpu.SemaphoreType.DMA((columns, CORES)),
        ],
        compiler_params=pltpu.CompilerParams(vmem_limit_bytes=44 * 1024 * 1024),
        cost_estimate=pl.CostEstimate(
            flops=total * features, bytes_accessed=total * features, transcendentals=0
        ),
    )(meta, slot_rows, slot_gates, *flat, *weights)


def add(*values):
    return sum(value.astype(F32) for value in values).astype(BF16)


def after(value, *events):
    return lax.optimization_barrier((value, *events))[0]


def staged(hidden, gate_weight, up_weight, down_weight, block_rows, slot_gate, parts):
    rows_here, features = hidden.shape[2], hidden.shape[3]
    slots = block_rows.shape[2] * block_rows.shape[3]
    index = lax.axis_index("tensor")
    core, chip = index % CORES, index // CORES
    right = chip >= CHIPS // 2
    inner = jnp.logical_and(chip > 0, chip < CHIPS - 1).astype(jnp.int32)

    mine = lax.dynamic_index_in_dim(hidden[0], core, 0, keepdims=False)
    theirs = lax.dynamic_index_in_dim(hidden[0], 1 - core, 0, keepdims=False)
    slot_rows = lax.dynamic_index_in_dim(block_rows[0], core, 0, keepdims=False).reshape(1, slots)
    slot_gates = lax.dynamic_index_in_dim(slot_gate[0], core, 0, keepdims=False).reshape(1, slots)

    other = across_cores(theirs)
    other, *own_weights = lax.optimization_barrier(
        (other, gate_weight[0], up_weight[0], down_weight[0])
    )
    weights = own_weights + [across_cores(weight) for weight in own_weights]

    chunks = []
    for half, sizes in enumerate(parts):
        start = 0
        for size in sizes:
            chunks.append((half, start, size))
            start += size
    pieces = [
        (mine if half == 0 else other)[start : start + size] for half, start, size in chunks
    ]
    last = len(chunks)
    at_inner = inner == 1

    def meta_of(runs):
        values = [inner]
        for mirrored_block, chunk in runs:
            half, start, _ = chunks[chunk]
            block = jnp.where(right, CHIPS - 1 - mirrored_block, mirrored_block)
            owner = block * CORES + (core if half == 0 else 1 - core)
            values.append(owner * rows_here + start)
        return jnp.stack(values).astype(jnp.int32)

    def expert(runs, inputs, out_rows):
        return ffn(meta_of(runs), slot_rows, slot_gates, inputs, weights, out_rows)

    near, second_in, third_in, second_out, third_out = ([None] * last for _ in range(5))
    for k in range(last):
        near[k] = along_line(pieces[k], NEAR)
    second_in[0] = along_line(after(pieces[0], other), MIDDLE)
    third_in[0] = along_line(after(near[0], second_in[0]), MIDDLE)
    second_out[0] = along_line(after(second_in[0], near[0]), NEAR)

    ready = [third_in[0]] + near[1:]
    near_in = [after(pieces[0], second_out[0], *ready)] + pieces[1:]
    out = expert(
        [(inner, k) for k in range(last)] + [(1 - inner, k) for k in range(last)],
        [(piece,) for piece in near_in] + [(value,) for value in near],
        [chunk[2] for chunk in chunks] * 2,
    )
    own_part, near_part = out[:last], out[last:]
    third_out[0] = along_line(after(third_in[0], *near), NEAR)
    for k in range(1, last):
        if k > 1:
            ready = [third_in[k - 1]]
        second_in[k] = along_line(after(pieces[k], *ready), MIDDLE)
        third_in[k] = along_line(after(near[k], *ready), MIDDLE)
        second_out[k] = along_line(after(second_in[k], own_part[0]), OUTWARD)
        third_out[k] = along_line(after(third_in[k], own_part[0]), OUTWARD)

    base = [
        to_next_phase(
            jnp.concatenate(
                [add(pieces[k], own_part[k]) for k in range(last) if chunks[k][0] == half]
            ),
            STAY,
            half,
        )
        for half in range(CORES)
    ]

    handed = [[], []]
    over = to_pair = None
    for k, (half, start, size) in enumerate(chunks):
        events = [own_part[0]]
        if k + 1 < last:
            events += [second_in[k + 1], third_in[k + 1]]
        inputs = [
            (after(second_out[k], *events), second_in[k]),
            (third_out[k], third_in[k]),
        ]
        if k + 1 < last:
            part = expert([(2, k), (3, k)], inputs, [2 * size])[0]
            total = add(part, along_line(part, INWARD))
            sum2, sum3 = total[:size], total[size:]
        else:
            part2, part3 = expert([(2, k), (3, k)], inputs, [size, size])
            sum3 = add(part3, along_line(part3, INWARD))
            if k > 0:
                part2, sum3 = after(part2, over), after(sum3, for_pair)
            sum2 = add(part2, along_line(part2, INWARD))
        sum2 = jnp.where(at_inner, sum2, 0)
        over = along_line(sum3, MIDDLE)
        for_pair = add(near_part[k], jnp.where(at_inner, over, 0))
        if k > 0:
            for_pair = after(for_pair, to_pair)
        to_pair = to_next_phase(for_pair, NEAR, half)
        handed[half].append(
            add(
                base[half][start : start + size],
                to_next_phase(sum2, MIDDLE + ENDS, half),
                to_pair,
            )
        )
    same, cross = (jnp.concatenate(half, axis=0) for half in handed)
    low = core == 0
    return jnp.stack([jnp.where(low, same, cross), jnp.where(low, cross, same)])[None]


def whole_gather(hidden, gate_weight, up_weight, down_weight, block_rows, slot_gate):
    rows_here = hidden.shape[2]
    slots = block_rows.shape[2] * block_rows.shape[3]
    total_rows = rows_here * lax.axis_size("tensor")
    gathered = lax.all_gather(hidden, "tensor", axis=2, tiled=True)
    results = []
    for micro_batch in range(hidden.shape[1]):
        x = gathered[0, micro_batch]
        slot_rows = block_rows[0, micro_batch].reshape(1, slots)
        slot_gates = slot_gate[0, micro_batch].reshape(1, slots)
        tokens = lax.broadcasted_iota(jnp.int32, (total_rows, 1), 0)
        gate = jnp.sum(jnp.where(slot_rows == tokens, slot_gates, 0.0), axis=1, keepdims=True)
        gate_act = jnp.dot(x, gate_weight[0], preferred_element_type=F32)
        up_act = jnp.dot(x, up_weight[0], preferred_element_type=F32)
        hidden_act = (jax.nn.silu(gate_act) * up_act).astype(BF16)
        part = jnp.dot(hidden_act, down_weight[0], preferred_element_type=F32) * gate
        placed = lax.psum_scatter(
            part.astype(BF16), "tensor", scatter_dimension=0, tiled=True
        )
        results.append(add(hidden[0, micro_batch], placed))
    count = lax.axis_size("segment")
    pairs = [(source, (source + 1) % count) for source in range(count)]
    return lax.ppermute(jnp.stack(results)[None], "segment", pairs)


def per_device(*args):
    rows_here = args[0].shape[2]
    if (
        lax.axis_size("tensor") != CORES * CHIPS
        or args[0].shape[1] != CORES
        or rows_here % 32 != 0
    ):
        return whole_gather(*args)
    return staged(*args, parts=[[rows_here], [rows_here]])


def solution(mesh):
    return jax.shard_map(
        per_device,
        mesh=mesh,
        in_specs=(
            P("segment", None, "tensor", None),
            P("segment", None, "tensor"),
            P("segment", None, "tensor"),
            P("segment", "tensor", None),
            P("segment", None, None, None),
            P("segment", None, None, None),
        ),
        out_specs=P("segment", None, "tensor", None),
        check_vma=False,
    )
```

```python
import functools

import jax
import jax.numpy as jnp
from jax import lax
from jax.experimental import pallas as pl
from jax.experimental.pallas import tpu as pltpu
from jax.sharding import PartitionSpec as P

CORES = 2
VMEM_LIMIT = 14 * 1024 * 1024
CHIPS = 4
BF16 = jnp.bfloat16
F32 = jnp.float32

NEAR = [(0, 1), (1, 0), (2, 3), (3, 2)]
MIDDLE = [(1, 2), (2, 1)]
STAY = [(0, 0), (1, 1), (2, 2), (3, 3)]


def along_line(value, pairs):
    full = [(CORES * a + c, CORES * b + c) for a, b in pairs for c in range(CORES)]
    return lax.ppermute(value, "tensor", full)


def across_cores(value):
    count = lax.axis_size("tensor")
    return lax.ppermute(value, "tensor", [(i, i ^ 1) for i in range(count)])


def to_next_phase(value, pairs, cross):
    segments, count = lax.axis_size("segment"), lax.axis_size("tensor")
    full = [
        (s * count + CORES * a + c, ((s + 1) % segments) * count + CORES * b + (c ^ cross))
        for s in range(segments)
        for a, b in pairs
        for c in range(CORES)
    ]
    return lax.ppermute(value, ("segment", "tensor"), full)


def ffn_kernel(layout, out_rows, *refs):
    n_in = sum(choices for choices, _ in layout)
    n_out = len(out_rows)
    meta, slot_rows, slot_gates = refs[:3]
    x_refs = refs[3 : 3 + n_in]
    weights = refs[3 + n_in : 9 + n_in]
    outs = refs[9 + n_in : 9 + n_in + n_out]
    x, h, gate = refs[9 + n_in + n_out :]
    hidden_units, features = weights[2].shape

    second = meta[0] == 1
    start = at = run = 0
    for choices, runs in layout:
        here = pl.ds(start, sum(runs))
        if choices == 1:
            x[here, :] = x_refs[at][...]
        else:
            first_ref, second_ref = x_refs[at], x_refs[at + 1]

            @pl.when(second)
            def _(here=here, ref=second_ref):
                x[here, :] = ref[...]

            @pl.when(jnp.logical_not(second))
            def _(here=here, ref=first_ref):
                x[here, :] = ref[...]

        at += choices
        for rows in runs:
            tokens = meta[1 + run] + lax.broadcasted_iota(
                jnp.int32, (rows, slot_rows.shape[1]), 0
            )
            named = jnp.where(slot_rows[...] == tokens, slot_gates[...], 0.0)
            column = jnp.sum(named, axis=1, keepdims=True)
            gate[pl.ds(start, rows), :] = jnp.broadcast_to(column, (rows, gate.shape[1]))
            start += rows
            run += 1

    width = 256 if hidden_units % 256 == 0 else hidden_units
    for core in range(CORES):
        for begin in range(0, hidden_units, width):
            g = jnp.dot(x[...], weights[3 * core][:, begin : begin + width], preferred_element_type=F32)
            u = jnp.dot(x[...], weights[3 * core + 1][:, begin : begin + width], preferred_element_type=F32)
            at = core * hidden_units + begin
            h[:, at : at + width] = (g / (1.0 + jnp.exp(-g)) * u).astype(BF16)
    out_width = 768 if features % 768 == 0 else features
    for begin in range(0, features, out_width):
        span = slice(begin, begin + out_width)
        y = jnp.dot(h[:, :hidden_units], weights[2][:, span], preferred_element_type=F32)
        y += jnp.dot(h[:, hidden_units:], weights[5][:, span], preferred_element_type=F32)
        y = (y * gate[:, :1]).astype(BF16)
        start = 0
        for rows, out in zip(out_rows, outs):
            out[:, span] = y[start : start + rows, :]
            start += rows


def ffn(meta, slot_rows, slot_gates, inputs, runs, weights, out_rows):
    layout = tuple((len(choice), rows) for choice, rows in zip(inputs, runs))
    features, hidden_units = weights[0].shape
    total = sum(out_rows)
    vmem = pl.BlockSpec(memory_space=pltpu.VMEM)
    flat = [value for choice in inputs for value in choice]
    return pl.pallas_call(
        functools.partial(ffn_kernel, layout, out_rows),
        out_shape=[jax.ShapeDtypeStruct((rows, features), BF16) for rows in out_rows],
        in_specs=[pl.BlockSpec(memory_space=pltpu.SMEM)] + [vmem] * (8 + len(flat)),
        out_specs=[vmem] * len(out_rows),
        scratch_shapes=[
            pltpu.VMEM((total, features), BF16),
            pltpu.VMEM((total, CORES * hidden_units), BF16),
            pltpu.VMEM((total, 128), F32),
        ],
        compiler_params=pltpu.CompilerParams(vmem_limit_bytes=VMEM_LIMIT),
        cost_estimate=pl.CostEstimate(
            flops=24 * 10**6 * total, bytes_accessed=0, transcendentals=0
        ),
    )(meta, slot_rows, slot_gates, *flat, *weights)


def add(*values):
    return sum(value.astype(F32) for value in values).astype(BF16)


def after(value, *events):
    return lax.optimization_barrier((value, *events))[0]


def staged(hidden, gate_weight, up_weight, down_weight, block_rows, slot_gate, parts):
    rows_here, features = hidden.shape[2], hidden.shape[3]
    slots = block_rows.shape[2] * block_rows.shape[3]
    index = lax.axis_index("tensor")
    core, chip = index % CORES, index // CORES
    right = chip >= CHIPS // 2
    inner = jnp.logical_and(chip > 0, chip < CHIPS - 1).astype(jnp.int32)

    mine = lax.dynamic_index_in_dim(hidden[0], core, 0, keepdims=False)
    theirs = lax.dynamic_index_in_dim(hidden[0], 1 - core, 0, keepdims=False)
    mine = lax.optimization_barrier(mine)
    slot_rows = lax.dynamic_index_in_dim(block_rows[0], core, 0, keepdims=False).reshape(1, slots)
    slot_gates = lax.dynamic_index_in_dim(slot_gate[0], core, 0, keepdims=False).reshape(1, slots)

    chunks = []
    for half, sizes in enumerate(parts):
        start = 0
        for size in sizes:
            chunks.append((half, start, size))
            start += size
    last = len(chunks)

    def meta_of(runs):
        values = [inner]
        for mirrored_block, chunk in runs:
            half, start, _ = chunks[chunk]
            block = jnp.where(right, CHIPS - 1 - mirrored_block, mirrored_block)
            owner = block * CORES + (core if half == 0 else 1 - core)
            values.append(owner * rows_here + start)
        return jnp.stack(values).astype(jnp.int32)

    every, own_block = range(last), [inner, 1 - inner]
    metas = [meta_of([(block, k) for block in own_block for k in every])]
    metas += [meta_of([(2, k), (3, k)]) for k in every]
    low, at_inner = core == 0, inner == 1
    other, own_weights, metas, low, at_inner, slot_rows, slot_gates = lax.optimization_barrier(
        (
            across_cores(theirs),
            [gate_weight[0], up_weight[0], down_weight[0]],
            metas,
            low,
            at_inner,
            slot_rows,
            slot_gates,
        )
    )
    pieces = [
        (mine if half == 0 else other)[start : start + size] for half, start, size in chunks
    ]

    sizes = [size for _, _, size in chunks]

    near = [along_line(pieces[0], NEAR)]
    rest = along_line(jnp.concatenate(pieces[1:], axis=0), NEAR)
    start = 0
    for size in sizes[1:]:
        near.append(rest[start : start + size])
        start += size
    weights = own_weights + [across_cores(weight) for weight in own_weights]

    def expert(meta, inputs, runs, out_rows):
        return list(ffn(meta, slot_rows, slot_gates, inputs, runs, weights, out_rows))

    across = [
        along_line(jnp.concatenate([piece, value], axis=0), MIDDLE)
        for piece, value in zip(pieces, near)
    ]

    def exchange(k):
        if k < 2:
            payload = across[k]
        elif k < last:
            payload = jnp.where(at_inner, across[k], parts_far[k - 2])
        else:
            payload = parts_far[k - 2]
        return along_line(payload, NEAR)

    parts_far, swapped, over = [], [exchange(0)], []
    for k in range(1, last + 2):
        swapped.append(exchange(k))
        j = k - 1
        if j < last:
            events = parts_far[j - 1 : j]
            if j == 1:
                ready = [after(pieces[0], *events)] + pieces[1:] + near
                out = expert(
                    metas[0], [(value,) for value in ready], [[n] for n in sizes * 2], sizes * 2
                )
                own_part, near_part = out[:last], out[last:]
                events = events + own_part[:1]
            if j == last - 1:
                events = events + over[:1]
            rows = (after(swapped[j], *events), across[j])
            parts_far += expert(metas[1 + j], [rows], [[sizes[j]] * 2], [2 * sizes[j]])
        if k >= 2:
            j = k - 2
            total = add(parts_far[j], swapped[k])
            if j + 1 < last:
                total = after(total, parts_far[j + 1])
            if j > 0:
                total = after(total, over[max(j - 2, 0)])
            over.append(along_line(total, MIDDLE))

    handed, sent = [[], []], []
    for k, (half, _, size) in enumerate(chunks):
        for_pair = add(near_part[k], over[k][size:])
        if k > 1:
            for_pair = after(for_pair, sent[k - 2])
        from_pair = along_line(for_pair, NEAR)
        done = add(pieces[k], own_part[k], over[k][:size], from_pair)
        sent.append(to_next_phase(done, STAY, half))
        handed[half].append(sent[k])
    same, cross = (jnp.concatenate(half, axis=0) for half in handed)
    return jnp.stack([jnp.where(low, same, cross), jnp.where(low, cross, same)])[None]


def whole_gather(hidden, gate_weight, up_weight, down_weight, block_rows, slot_gate):
    rows_here = hidden.shape[2]
    slots = block_rows.shape[2] * block_rows.shape[3]
    total_rows = rows_here * lax.axis_size("tensor")
    gathered = lax.all_gather(hidden, "tensor", axis=2, tiled=True)
    results = []
    for micro_batch in range(hidden.shape[1]):
        x = gathered[0, micro_batch]
        slot_rows = block_rows[0, micro_batch].reshape(1, slots)
        slot_gates = slot_gate[0, micro_batch].reshape(1, slots)
        tokens = lax.broadcasted_iota(jnp.int32, (total_rows, 1), 0)
        gate = jnp.sum(jnp.where(slot_rows == tokens, slot_gates, 0.0), axis=1, keepdims=True)
        gate_act = jnp.dot(x, gate_weight[0], preferred_element_type=F32)
        up_act = jnp.dot(x, up_weight[0], preferred_element_type=F32)
        hidden_act = (jax.nn.silu(gate_act) * up_act).astype(BF16)
        part = jnp.dot(hidden_act, down_weight[0], preferred_element_type=F32) * gate
        placed = lax.psum_scatter(
            part.astype(BF16), "tensor", scatter_dimension=0, tiled=True
        )
        results.append(add(hidden[0, micro_batch], placed))
    count = lax.axis_size("segment")
    pairs = [(source, (source + 1) % count) for source in range(count)]
    return lax.ppermute(jnp.stack(results)[None], "segment", pairs)


def per_device(*args):
    rows_here = args[0].shape[2]
    if (
        lax.axis_size("tensor") != CORES * CHIPS
        or args[0].shape[1] != CORES
        or rows_here % 32 != 0
    ):
        return whole_gather(*args)
    return staged(*args, parts=[[rows_here // 2] * 2] * 2)


def solution(mesh):
    return jax.shard_map(
        per_device,
        mesh=mesh,
        in_specs=(
            P("segment", None, "tensor", None),
            P("segment", None, "tensor"),
            P("segment", None, "tensor"),
            P("segment", "tensor", None),
            P("segment", None, None, None),
            P("segment", None, None, None),
        ),
        out_specs=P("segment", None, "tensor", None),
        check_vma=False,
    )
```

```python
import functools

import jax
import jax.numpy as jnp
from jax import lax
from jax.experimental import pallas as pl
from jax.experimental.pallas import tpu as pltpu
from jax.sharding import PartitionSpec as P

CORES = 2
VMEM_LIMIT = 14 * 1024 * 1024
CHIPS = 4
BF16 = jnp.bfloat16
F32 = jnp.float32

NEAR = [(0, 1), (1, 0), (2, 3), (3, 2)]
MIDDLE = [(1, 2), (2, 1)]
STAY = [(0, 0), (1, 1), (2, 2), (3, 3)]


def along_line(value, pairs):
    full = [(CORES * a + c, CORES * b + c) for a, b in pairs for c in range(CORES)]
    return lax.ppermute(value, "tensor", full)


def across_middle(value):
    inside = [(CORES * a + c, CORES * b + c) for a, b in MIDDLE for c in range(CORES)]
    ends = [(CORES * a + c, CORES * a + 1 - c) for a in (0, CHIPS - 1) for c in range(CORES)]
    return lax.ppermute(value, "tensor", inside + ends)


def across_cores(value):
    count = lax.axis_size("tensor")
    return lax.ppermute(value, "tensor", [(i, i ^ 1) for i in range(count)])


def to_next_phase(value, pairs, cross):
    segments, count = lax.axis_size("segment"), lax.axis_size("tensor")
    full = [
        (s * count + CORES * a + c, ((s + 1) % segments) * count + CORES * b + (c ^ cross))
        for s in range(segments)
        for a, b in pairs
        for c in range(CORES)
    ]
    return lax.ppermute(value, ("segment", "tensor"), full)


def ffn_kernel(layout, out_rows, *refs):
    n_in = sum(choices for choices, _ in layout)
    n_out = len(out_rows)
    meta, slot_rows, slot_gates = refs[:3]
    x_refs = refs[3 : 3 + n_in]
    weights = refs[3 + n_in : 9 + n_in]
    outs = refs[9 + n_in : 9 + n_in + n_out]
    x, h, gate = refs[9 + n_in + n_out :]
    hidden_units, features = weights[2].shape

    second = meta[0] == 1
    start = at = run = 0
    for choices, runs in layout:
        here = pl.ds(start, sum(runs))
        if choices == 1:
            x[here, :] = x_refs[at][...]
        else:
            first_ref, second_ref = x_refs[at], x_refs[at + 1]

            @pl.when(second)
            def _(here=here, ref=second_ref):
                x[here, :] = ref[...]

            @pl.when(jnp.logical_not(second))
            def _(here=here, ref=first_ref):
                x[here, :] = ref[...]

        at += choices
        for rows in runs:
            tokens = meta[1 + run] + lax.broadcasted_iota(
                jnp.int32, (rows, slot_rows.shape[1]), 0
            )
            named = jnp.where(slot_rows[...] == tokens, slot_gates[...], 0.0)
            column = jnp.sum(named, axis=1, keepdims=True)
            gate[pl.ds(start, rows), :] = jnp.broadcast_to(column, (rows, gate.shape[1]))
            start += rows
            run += 1

    width = 256 if hidden_units % 256 == 0 else hidden_units
    for core in range(CORES):
        for begin in range(0, hidden_units, width):
            g = jnp.dot(x[...], weights[3 * core][:, begin : begin + width], preferred_element_type=F32)
            u = jnp.dot(x[...], weights[3 * core + 1][:, begin : begin + width], preferred_element_type=F32)
            at = core * hidden_units + begin
            h[:, at : at + width] = (g / (1.0 + jnp.exp(-g)) * u).astype(BF16)
    out_width = 768 if features % 768 == 0 else features
    for begin in range(0, features, out_width):
        span = slice(begin, begin + out_width)
        y = jnp.dot(h[:, :hidden_units], weights[2][:, span], preferred_element_type=F32)
        y += jnp.dot(h[:, hidden_units:], weights[5][:, span], preferred_element_type=F32)
        y = (y * gate[:, :1]).astype(BF16)
        start = 0
        for rows, out in zip(out_rows, outs):
            out[:, span] = y[start : start + rows, :]
            start += rows


def ffn(meta, slot_rows, slot_gates, inputs, runs, weights, out_rows):
    layout = tuple((len(choice), rows) for choice, rows in zip(inputs, runs))
    features, hidden_units = weights[0].shape
    total = sum(out_rows)
    vmem = pl.BlockSpec(memory_space=pltpu.VMEM)
    flat = [value for choice in inputs for value in choice]
    return pl.pallas_call(
        functools.partial(ffn_kernel, layout, out_rows),
        out_shape=[jax.ShapeDtypeStruct((rows, features), BF16) for rows in out_rows],
        in_specs=[pl.BlockSpec(memory_space=pltpu.SMEM)] + [vmem] * (8 + len(flat)),
        out_specs=[vmem] * len(out_rows),
        scratch_shapes=[
            pltpu.VMEM((total, features), BF16),
            pltpu.VMEM((total, CORES * hidden_units), BF16),
            pltpu.VMEM((total, 128), F32),
        ],
        compiler_params=pltpu.CompilerParams(vmem_limit_bytes=VMEM_LIMIT),
        cost_estimate=pl.CostEstimate(
            flops=24 * 10**6 * total, bytes_accessed=0, transcendentals=0
        ),
    )(meta, slot_rows, slot_gates, *flat, *weights)


def add(*values):
    return sum(value.astype(F32) for value in values).astype(BF16)


def after(value, *events):
    return lax.optimization_barrier((value, *events))[0]


def staged(hidden, gate_weight, up_weight, down_weight, block_rows, slot_gate, parts):
    rows_here, features = hidden.shape[2], hidden.shape[3]
    slots = block_rows.shape[2] * block_rows.shape[3]
    index = lax.axis_index("tensor")
    core, chip = index % CORES, index // CORES
    right = chip >= CHIPS // 2
    inner = jnp.logical_and(chip > 0, chip < CHIPS - 1).astype(jnp.int32)

    mine = lax.dynamic_index_in_dim(hidden[0], core, 0, keepdims=False)
    theirs = lax.dynamic_index_in_dim(hidden[0], 1 - core, 0, keepdims=False)
    mine = lax.optimization_barrier(mine)
    slot_rows = lax.dynamic_index_in_dim(block_rows[0], core, 0, keepdims=False).reshape(1, slots)
    slot_gates = lax.dynamic_index_in_dim(slot_gate[0], core, 0, keepdims=False).reshape(1, slots)

    chunks = []
    for half, sizes in enumerate(parts):
        start = 0
        for size in sizes:
            chunks.append((half, start, size))
            start += size
    last = len(chunks)

    def meta_of(runs):
        values = [inner]
        for mirrored_block, chunk in runs:
            half, start, _ = chunks[chunk]
            block = jnp.where(right, CHIPS - 1 - mirrored_block, mirrored_block)
            owner = block * CORES + (core if half == 0 else 1 - core)
            values.append(owner * rows_here + start)
        return jnp.stack(values).astype(jnp.int32)

    every, own_block = range(last), [inner, 1 - inner]
    metas = [meta_of([(block, k) for block in own_block for k in every])]
    metas += [meta_of([(2, k), (3, k)]) for k in every]
    low, at_inner = core == 0, inner == 1
    other, own_weights, metas, low, at_inner, slot_rows, slot_gates = lax.optimization_barrier(
        (
            across_cores(theirs),
            [gate_weight[0], up_weight[0], down_weight[0]],
            metas,
            low,
            at_inner,
            slot_rows,
            slot_gates,
        )
    )
    pieces = [
        (mine if half == 0 else other)[start : start + size] for half, start, size in chunks
    ]

    sizes = [size for _, _, size in chunks]

    near = [along_line(pieces[0], NEAR)]
    rest = along_line(jnp.concatenate(pieces[1:], axis=0), NEAR)
    start = 0
    for size in sizes[1:]:
        near.append(rest[start : start + size])
        start += size
    weights = own_weights + [across_cores(weight) for weight in own_weights]

    def expert(meta, inputs, runs, out_rows):
        return list(ffn(meta, slot_rows, slot_gates, inputs, runs, weights, out_rows))

    across = [
        across_middle(jnp.concatenate([piece, value], axis=0))
        for piece, value in zip(pieces, near)
    ]

    def exchange(k):
        if k < 2:
            payload = across[k]
        elif k < last:
            payload = jnp.where(at_inner, across[k], parts_far[k - 2])
        else:
            payload = parts_far[k - 2]
        return along_line(payload, NEAR)

    parts_far, swapped, over = [], [exchange(0)], []
    for k in range(1, last + 2):
        swapped.append(exchange(k))
        j = k - 1
        if j < last:
            events = parts_far[j - 1 : j]
            if j == 1:
                ready = [after(pieces[0], *events)] + pieces[1:] + near
                out = expert(
                    metas[0], [(value,) for value in ready], [[n] for n in sizes * 2], sizes * 2
                )
                own_part, near_part = out[:last], out[last:]
                events = events + own_part[:1]
            if j == last - 1:
                events = events + over[:1]
            rows = (after(swapped[j], *events), across[j])
            parts_far += expert(metas[1 + j], [rows], [[sizes[j]] * 2], [2 * sizes[j]])
        if k >= 2:
            j = k - 2
            total = add(parts_far[j], swapped[k])
            if j + 1 < last:
                total = after(total, parts_far[j + 1])
            if j > 0:
                total = after(total, over[max(j - 2, 0)])
            over.append(jnp.where(at_inner, across_middle(total), 0))

    handed, sent = [[], []], []
    for k, (half, _, size) in enumerate(chunks):
        for_pair = add(near_part[k], over[k][size:])
        if k == last - 1:
            for_pair = after(for_pair, sent[0])
        from_pair = along_line(for_pair, NEAR)
        done = add(pieces[k], own_part[k], over[k][:size], from_pair)
        if k == last - 1:
            done = after(done, sent[1])
        sent.append(to_next_phase(done, STAY, half))
        handed[half].append(sent[k])
    same, cross = (jnp.concatenate(half, axis=0) for half in handed)
    return jnp.stack([jnp.where(low, same, cross), jnp.where(low, cross, same)])[None]


def whole_gather(hidden, gate_weight, up_weight, down_weight, block_rows, slot_gate):
    rows_here = hidden.shape[2]
    slots = block_rows.shape[2] * block_rows.shape[3]
    total_rows = rows_here * lax.axis_size("tensor")
    gathered = lax.all_gather(hidden, "tensor", axis=2, tiled=True)
    results = []
    for micro_batch in range(hidden.shape[1]):
        x = gathered[0, micro_batch]
        slot_rows = block_rows[0, micro_batch].reshape(1, slots)
        slot_gates = slot_gate[0, micro_batch].reshape(1, slots)
        tokens = lax.broadcasted_iota(jnp.int32, (total_rows, 1), 0)
        gate = jnp.sum(jnp.where(slot_rows == tokens, slot_gates, 0.0), axis=1, keepdims=True)
        gate_act = jnp.dot(x, gate_weight[0], preferred_element_type=F32)
        up_act = jnp.dot(x, up_weight[0], preferred_element_type=F32)
        hidden_act = (jax.nn.silu(gate_act) * up_act).astype(BF16)
        part = jnp.dot(hidden_act, down_weight[0], preferred_element_type=F32) * gate
        placed = lax.psum_scatter(
            part.astype(BF16), "tensor", scatter_dimension=0, tiled=True
        )
        results.append(add(hidden[0, micro_batch], placed))
    count = lax.axis_size("segment")
    pairs = [(source, (source + 1) % count) for source in range(count)]
    return lax.ppermute(jnp.stack(results)[None], "segment", pairs)


def per_device(*args):
    rows_here = args[0].shape[2]
    if (
        lax.axis_size("tensor") != CORES * CHIPS
        or args[0].shape[1] != CORES
        or rows_here % 32 != 0
    ):
        return whole_gather(*args)
    return staged(*args, parts=[[rows_here // 2] * 2] * 2)


def solution(mesh):
    return jax.shard_map(
        per_device,
        mesh=mesh,
        in_specs=(
            P("segment", None, "tensor", None),
            P("segment", None, "tensor"),
            P("segment", None, "tensor"),
            P("segment", "tensor", None),
            P("segment", None, None, None),
            P("segment", None, None, None),
        ),
        out_specs=P("segment", None, "tensor", None),
        check_vma=False,
    )
```
